128 devices in a mesh: ha: 8 (over y_hi, z), wa: 16 (over x, y_lo, core).
Axes of the slice: x: 4, y: 4 (y_hi: 2, y_lo: 2; y = y_hi * 2 + y_lo), z: 4, core: 2. Of those that a mesh axis runs over, the one named last changes fastest.
Arguments:
- latent: bfloat16 [16, 64, 128, 1152], P(None, 'ha', 'wa'), may hold values from -6 to 6
- qkv_weight: bfloat16 [2, 1152, 3456], replicated, as said below
- proj_weight: bfloat16 [2, 1152, 1152], P(None, None, 'wa'), may hold values from -0.1875 to 0.1875
- modulation: float32 [2, 3, 1152], replicated, may hold values from -3 to 3
- regions: int32 [16, 64, 128], P(None, 'ha', 'wa'), may hold values from 0 to 2
- frame_shift: int32 [1], replicated, may hold values from 1 to 7
Outputs:
- result: bfloat16 [16, 64, 128, 1152], P(None, 'ha', 'wa')
The draws below stay inside these ranges and needn't reach their ends.
Inputs may be any that keep to these rules, and one draw needn't show every extreme that they name: `qkv_weight`: query, key and value projections, scaled by the inverse square root of 1152.
All inputs are finite; a program needn't handle non-finite values.
Results may differ from the reference program's by a relative error of at most 0.0055.
Values may be sent and summed in bfloat16 or wider, within the bound.
A program may use at most 192 MiB of HBM per device.

```python
import math
import jax
import jax.numpy as jnp
from jax import lax

D = 1152
HEADS = 16
WIN = 8
SHIFT = 4
NT = 16
NH = 64
NW = 128


def draw_qkv_weight(key, part):
    key = jax.random.fold_in(key, 5)
    first_key, second_key, third_key = jax.random.split(key, 3)
    base = jax.random.normal(first_key, (2, D, D), jnp.float32)
    noise = jax.random.normal(second_key, (2, D, D), jnp.float32)
    query_part = base
    key_part = noise
    value_part = jax.random.normal(third_key, (2, D, D), jnp.float32)
    joined = jnp.concatenate([query_part, key_part, value_part], axis=2) / jnp.sqrt(jnp.float32(D))
    return joined.astype(jnp.bfloat16)


def plant(values, key, least, top_value):
    longest = values.shape.index(max(values.shape))
    spots = []
    for shift in (0, 1):
        where = [jax.random.randint(jax.random.fold_in(key, axis), (), 0, length) for axis, length in enumerate(values.shape)]
        where[longest] = (where[longest] + shift) % values.shape[longest]
        spots.append(tuple(where))
    return values.at[spots[0]].set(least).at[spots[1]].set(top_value)


def shard_levels(own_key, dims, pieces, least, largest):
    gain, own = 1.0, jax.random.fold_in(own_key, 6)
    for position, shards_of in pieces:
        steps = jnp.exp(jax.random.uniform(jax.random.fold_in(own, position), (shards_of,), jnp.float32, least / len(pieces), largest / len(pieces)))
        gain = gain * jnp.repeat(steps, dims[position] // shards_of).reshape([-1 if axis == position else 1 for axis in range(len(dims))])
    return gain


def bell_draw(own_key, dims, scale, reach, pieces=(), kind=jnp.bfloat16):
    drawn = scale * jax.random.normal(own_key, dims, jnp.float32)
    if pieces:
        drawn = drawn * shard_levels(own_key, dims, pieces, -0.22, 0.18)
    return jnp.clip(drawn, -reach, reach).astype(kind)


def setup_inputs(seed: int = 0) -> dict:
    key_list = jax.random.split(jax.random.key(seed), 7)
    latent = bell_draw(key_list[0], (NT, NH, NW, D), 1.0, 6.0, ((1, 8), (2, 16)))
    qkv_weight = draw_qkv_weight(jax.random.fold_in(key_list[6], 71), 0)
    proj_weight = bell_draw(key_list[2], (2, D, D), D ** -0.5, 0.1875, ((2, 16),))
    modulation = bell_draw(key_list[3], (2, 3, D), 0.5, 3.0, (), jnp.float32)
    regions = plant(jax.random.randint(key_list[4], (NT, NH, NW), 0, 3), jax.random.fold_in(key_list[4], 1), 0, 2).astype(jnp.int32)
    frame_shift = jax.random.randint(key_list[5], (1,), 1, WIN).astype(jnp.int32)
    return dict(latent=latent, qkv_weight=qkv_weight, proj_weight=proj_weight, modulation=modulation, regions=regions, frame_shift=frame_shift)


def to_windows(grid):
    frames, height, width_cells = (grid.shape[0], grid.shape[1], grid.shape[2])
    tail_shape = grid.shape[3:]
    extra_axes = tuple(range(6, 6 + len(tail_shape)))
    split_shape = (frames // WIN, WIN, height // WIN, WIN, width_cells // WIN, WIN) + tail_shape
    reordered = grid.reshape(split_shape).transpose((0, 2, 4, 1, 3, 5) + extra_axes)
    return reordered.reshape((-1, WIN * WIN * WIN) + tail_shape)

def from_windows(stack, frames, height, width_cells):
    tail_shape = stack.shape[2:]
    extra_axes = tuple(range(6, 6 + len(tail_shape)))
    split_shape = (frames // WIN, height // WIN, width_cells // WIN, WIN, WIN, WIN) + tail_shape
    reordered = stack.reshape(split_shape).transpose((0, 3, 1, 4, 2, 5) + extra_axes)
    return reordered.reshape((frames, height, width_cells) + tail_shape)

def window_block(tokens, qkv_weight, proj_weight, modulate, region_map):
    frames, height, width_cells = (tokens.shape[0], tokens.shape[1], tokens.shape[2])
    values_f = tokens.astype(jnp.float32)
    center = lax.optimization_barrier(jnp.mean(values_f, -1, keepdims=True))
    spread = lax.optimization_barrier(jnp.mean(jnp.square(values_f - center), -1, keepdims=True))
    normed = (values_f - center) * lax.rsqrt(spread + 1e-06)
    scaled = (normed * (1.0 + modulate[1]) + modulate[0]).astype(jnp.bfloat16)
    windows_in = to_windows(scaled)
    windows_id = to_windows(region_map)

    def attend(pair):
        rows_in, labels = pair
        triple = jnp.dot(rows_in, qkv_weight, preferred_element_type=jnp.float32).astype(jnp.bfloat16)
        length = rows_in.shape[0]
        split_heads = triple.reshape(length, 3, HEADS, -1)
        query = split_heads[:, 0].astype(jnp.float32)
        keys = split_heads[:, 1].astype(jnp.float32)
        values = split_heads[:, 2].astype(jnp.float32)
        scale_factor = 1.0 / math.sqrt(query.shape[-1])
        scores = jnp.einsum('qhd,khd->hqk', query, keys) * scale_factor
        allowed = labels[:, None] == labels[None, :]
        scores = jnp.where(allowed[None], scores, -jnp.inf)
        peak = lax.optimization_barrier(jnp.max(scores, -1, keepdims=True))
        expo = jnp.exp(scores - peak)
        total = lax.optimization_barrier(jnp.sum(expo, -1, keepdims=True))
        weights = (expo / total).astype(jnp.bfloat16)
        mixed = jnp.einsum('hqk,khd->qhd', weights.astype(jnp.float32), values)
        mixed = mixed.astype(jnp.bfloat16).reshape(length, -1)
        return jnp.dot(mixed, proj_weight, preferred_element_type=jnp.float32)
    branch = lax.map(attend, (windows_in, windows_id))
    grid_branch = from_windows(branch, frames, height, width_cells)
    return (values_f + modulate[2] * grid_branch).astype(jnp.bfloat16)

def region_band(places, count, cut):
    return (places >= count - WIN).astype(jnp.int32) + (places >= count - cut).astype(jnp.int32)

def wrap_regions(frames_at, rows_at, cols_at, frames, total_rows, total_cols, offset):
    band_t = region_band(frames_at, frames, offset)
    band_h = region_band(rows_at, total_rows, SHIFT)
    band_w = region_band(cols_at, total_cols, SHIFT)
    return band_t[:, None, None] * 9 + band_h[None, :, None] * 3 + band_w[None, None, :]

def reference(latent, qkv_weight, proj_weight, modulation, regions, frame_shift):
    first = window_block(latent, qkv_weight[0], proj_weight[0], modulation[0], regions)
    offset = frame_shift[0].astype(jnp.int32)
    rolled = jnp.roll(first, -offset, axis=0)
    rolled = jnp.roll(rolled, -SHIFT, axis=1)
    rolled = jnp.roll(rolled, -SHIFT, axis=2)
    frames_at = jnp.arange(NT, dtype=jnp.int32)
    rows_at = jnp.arange(NH, dtype=jnp.int32)
    cols_at = jnp.arange(NW, dtype=jnp.int32)
    labels = wrap_regions(frames_at, rows_at, cols_at, NT, NH, NW, offset)
    second = window_block(rolled, qkv_weight[1], proj_weight[1], modulation[1], labels)
    result = jnp.roll(second, SHIFT, axis=2)
    result = jnp.roll(result, SHIFT, axis=1)
    return jnp.roll(result, offset, axis=0)
```

```python
import functools
import math

import jax
import jax.numpy as jnp
from jax import lax
from jax.experimental import pallas as pl
from jax.experimental.pallas import tpu as pltpu
from jax.sharding import PartitionSpec as P

D = 1152
HEADS = 16
HD = 72
BIG = 1e30
SCALE = math.log2(math.e) / math.sqrt(HD)
F32 = jnp.float32
BF16 = jnp.bfloat16
MESH = pl.DeviceIdType.MESH
NT = (((1,), (1,)), ((), ()))

OWN, RIGHT, VERT, DIAG = range(4)


def quadrant_matrix(rowflag):
    out = lax.broadcasted_iota(jnp.int32, (64, 64), 0)
    inn = lax.broadcasted_iota(jnp.int32, (64, 64), 1)
    role = out // 16
    outer = jnp.logical_or(role == OWN, role == DIAG)
    half_i = jnp.where(outer, rowflag, 1 - rowflag)
    half_j = 1 - role % 2
    row = half_i * 4 + (out % 16) // 4
    col = half_j * 4 + out % 4
    return jnp.where(inn == row * 8 + col, 1.0, 0.0)


def head_span(h):
    start = (HD * h) // 128 * 128
    offset = HD * h - start
    return start, offset, (128 if offset + HD <= 128 else 256)


def lane_row(width, low, high):
    lane = lax.broadcasted_iota(jnp.int32, (1, width), 1)
    return jnp.where(jnp.logical_and(lane >= low, lane < high), 1.0, 0.0).astype(BF16)


def layer_scale(x, m0, m1):
    center = jnp.mean(x, -1, keepdims=True)
    moved = x - center
    spread = jnp.mean(moved * moved, -1, keepdims=True)
    return (moved * lax.rsqrt(spread + 1e-6) * (1.0 + m1) + m0).astype(BF16)


def features(label, low):
    lane = lax.broadcasted_iota(jnp.int32, (512, 128), 1) - low
    inside = jnp.logical_and(lane >= 0, lane < 8)
    same = lane == label
    fq = jnp.where(jnp.logical_and(inside, same), 1.0, 0.0)
    fk = jnp.where(jnp.logical_and(inside, jnp.logical_not(same)), -BIG, 0.0)
    return fq.astype(BF16), fk.astype(BF16)


def attend(qkv, base, chunk, fq, fk, mixed):
    def scores(h):
        start, offset, width = head_span(h)
        side = 1 if offset == 0 else 0
        q = qkv[pl.ds(base + chunk * 16, 16), :, start : start + width].reshape(256, width)
        k = qkv[pl.ds(base, 32), :, D + start : D + start + width].reshape(512, width)
        mask = lane_row(width, offset, offset + HD)
        first = mask[:, :128]
        rows = slice(chunk * 256, chunk * 256 + 256)
        q0 = q[:, :128] * first + fq[side, rows]
        k = k * mask
        k0 = k[:, :128] + fk[side]
        if width == 256:
            q0 = jnp.concatenate([q0, q[:, 128:]], axis=1)
            k0 = jnp.concatenate([k0, k[:, 128:]], axis=1)
        return lax.dot_general(q0, k0, NT, preferred_element_type=F32)

    def values(h, s):
        start, offset, width = head_span(h)
        free = 127 if offset == 0 else 0
        s = s - jnp.max(s, axis=1, keepdims=True)
        weights = jnp.exp2(s).astype(BF16)
        v = qkv[pl.ds(base, 32), :, 2 * D + start : 2 * D + start + width].reshape(512, width)
        ones = lane_row(128, free, free + 1)
        v0 = v[:, :128] * (1.0 - ones) + ones
        if width == 256:
            v0 = jnp.concatenate([v0, v[:, 128:]], axis=1)
        out = jnp.dot(weights, v0, preferred_element_type=F32)
        out = out * (1.0 / out[:, free : free + 1])
        head = out[:, :128]
        if offset > 0:
            lane = lax.broadcasted_iota(jnp.int32, (256, 128), 1)
            head = jnp.where(lane >= offset, head, mixed[:, start : start + 128])
        mixed[:, start : start + 128] = head
        if width == 256:
            mixed[:, start + 128 : start + 256] = out[:, 128:]

    held = None
    for h in range(HEADS):
        s = scores(h)
        if held is not None:
            values(h - 1, held)
        held = s
    values(HEADS - 1, held)


def body(
    lat, weights, shard, mod, labels, shift,
    result,
    wbuf, x0, x1, scaled, qkv, rolled, mixed, first, second, feat_q, feat_k, sib, pairs,
    load_sem, sib_send, sib_recv, par_send, par_recv, rel_send, rel_recv,
    out_send, out_recv, back_send, back_recv, own_sem,
):
    ha, wa = lax.axis_index("ha"), lax.axis_index("wa")
    core = wa % 2
    ylo = (wa // 2) % 2
    xx = wa // 4
    chip = wa // 2
    rowflag = 1 - wa % 2
    down = 1 - 2 * (wa % 2)

    def at(h, w):
        return ((h + 8) % 8, (w + 16) % 16)

    sibling = at(ha, wa + 1 - 2 * core)

    def peer(k, sign):
        step = k + 1 if k < 3 else k - 3
        x = (xx + sign * step + 4) % 4
        y = ylo if k < 3 else 1 - ylo
        h = ha if k < 3 else (ha + 4) % 8
        return (h, (x * 2 + y) * 2 + core), x * 2 + y

    send_to = {RIGHT: at(ha, wa - 1), VERT: at(ha - down, wa), DIAG: at(ha + down, wa - 1)}
    back_to = {RIGHT: at(ha, wa + 1), VERT: at(ha + down, wa), DIAG: at(ha + down, wa + 1)}

    loads = []
    for b in range(2):
        for part in range(3):
            cols = pl.ds(part * D, D)
            loads.append(
                pltpu.make_async_copy(
                    weights.at[b, :, cols], wbuf.at[b, :, cols], load_sem.at[b, part]
                )
            )
    for copy in loads:
        copy.start()

    barrier = pltpu.get_barrier_semaphore()
    greet = [sibling] + [peer(k, -1)[0] for k in range(7)]
    greet += list(send_to.values()) + list(back_to.values())
    for device in greet:
        pl.semaphore_signal(barrier, inc=1, device_id=device, device_id_type=MESH)
    pl.semaphore_wait(barrier, len(greet))

    def remote(src, dst, send, recv, device):
        return pltpu.make_async_remote_copy(
            src_ref=src, dst_ref=dst, send_sem=send, recv_sem=recv,
            device_id=device, device_id_type=MESH,
        )

    swap = remote(shard, sib, sib_send, sib_recv, sibling)
    swap.start()

    pick = quadrant_matrix(rowflag).astype(BF16)

    def prepare(f, _):
        x = lat[f].astype(F32).reshape(64, D).astype(BF16)
        x = jnp.dot(pick, x, preferred_element_type=F32)
        y = layer_scale(x, mod[0, 0:1], mod[0, 1:2])
        x = x.astype(BF16)
        base = (f // 8) * 32 + f % 8
        for role in range(4):
            x0[base + role * 8] = x[role * 16 : role * 16 + 16]
            scaled[base + role * 8] = y[role * 16 : role * 16 + 16]
        return 0

    lax.fori_loop(0, 16, prepare, 0)

    swap.wait()
    for b in range(2):
        mine = shard[b].astype(F32)
        theirs = sib[b].astype(F32)
        low = jnp.where(core == 0, mine, theirs).T
        high = jnp.where(core == 0, theirs, mine).T
        pairs[b, chip] = jnp.concatenate([low, high], axis=0).astype(BF16)

    spans = ((0, 80), (80, 64))

    def parts(c, b):
        rows = pl.ds(*spans[c])
        out = []
        for k in range(7):
            device, _ = peer(k, 1)
            ref = pairs.at[b, chip, rows]
            out.append(remote(ref, ref, par_send.at[b, k], par_recv.at[b, k], device))
        return out

    def relays(c, b):
        rows = pl.ds(*spans[c])
        out = []
        for k in range(7):
            _, source = peer(k, -1)
            ref = pairs.at[b, source, rows]
            out.append(remote(ref, ref, rel_send.at[b, k], rel_recv.at[b, k], sibling))
        return out

    for c in range(2):
        @pl.when(core == c)
        def _():
            for b in range(2):
                for copy in parts(c, b):
                    copy.start()

    def pass_on(b):
        for c in range(2):
            @pl.when(core == c)
            def _():
                for copy, forward in zip(parts(c, b), relays(c, b)):
                    copy.wait_recv()
                    forward.start()

    def relayed(b):
        for c in range(2):
            @pl.when(core == c)
            def _():
                for forward in relays(1 - c, b):
                    forward.wait_recv()

    def triples(b, w):
        rows = scaled[pl.ds(w * 32, 32)].reshape(512, D)
        for part in range(3):
            cols = slice(part * D, part * D + D)
            out = jnp.dot(rows, wbuf[b, :, cols], preferred_element_type=F32)
            if part == 0:
                out = out * SCALE
            qkv[pl.ds(w * 32, 32), :, cols] = out.astype(BF16).reshape(32, 16, D)

    def project(b, x):
        w = pairs[b].reshape(D, D)
        branch = lax.dot_general(mixed[...].astype(BF16), w, NT, preferred_element_type=F32)
        return (x.astype(F32) + mod[b, 2:3] * branch).astype(BF16).reshape(16, 16, D)

    for copy in loads[:3]:
        copy.wait()

    def make0(w, _):
        triples(0, w)
        return 0

    lax.fori_loop(0, 2, make0, 0)
    pass_on(0)

    def exchange(w, role):
        place = pl.ds(w * 32 + role * 8, 8)
        return remote(
            first.at[place], x1.at[place], out_send.at[w, role - 1], out_recv.at[w, role - 1],
            send_to[role],
        )

    def block0(w, _):
        base = w * 32
        for side in range(2):
            feat_q[side] = labels[0, side, pl.ds(w * 512, 512)]
            feat_k[side] = labels[1, side, pl.ds(w * 512, 512)]
        for chunk in (1, 0):
            attend(qkv, base, chunk, feat_q, feat_k, mixed)
            if chunk == 1:
                @pl.when(w == 0)
                def _():
                    relayed(0)
            here = pl.ds(base + chunk * 16, 16)
            out = project(0, x0[here].reshape(256, D))
            if chunk == 1:
                first[here] = out
                exchange(w, DIAG).start()
                exchange(w, VERT).start()
            else:
                x1[pl.ds(base, 8)] = out[:8]
                first[pl.ds(base + 8, 8)] = out[8:]
                exchange(w, RIGHT).start()
        return 0

    lax.fori_loop(0, 2, block0, 0)
    pass_on(1)
    for copy in loads[3:]:
        copy.wait()

    def make1(w, _):
        for role in (RIGHT, VERT, DIAG):
            exchange(w, role).wait_recv()

        def norm(t, _):
            place = pl.ds(w * 32 + t * 4, 4)
            x = x1[place].reshape(64, D).astype(F32)
            scaled[place] = layer_scale(x, mod[1, 0:1], mod[1, 1:2]).reshape(4, 16, D)
            return 0

        lax.fori_loop(0, 8, norm, 0)
        triples(1, w)
        return 0

    lax.fori_loop(0, 2, make1, 0)
    relayed(1)

    offset = shift[0]
    row_block = (ha - wa % 2 + 8) % 8
    at_row_end = jnp.where(row_block == 7, 1, 0)
    at_col_end = jnp.where(wa == 15, 1, 0)

    def give_back(w, role):
        place = pl.ds(w * 32 + role * 8, 8)
        return remote(
            second.at[place], result.at[place], back_send.at[w, role - 1],
            back_recv.at[w, role - 1], back_to[role],
        )

    def keep(w):
        place = pl.ds(w * 32, 8)
        return pltpu.make_async_copy(second.at[place], result.at[place], own_sem.at[w])

    def block1(w, _):
        def roll(t, _):
            role, g = t // 8, t % 8
            frame = (w * 8 + g + offset) % 16
            rolled[t] = qkv[(frame // 8) * 32 + role * 8 + frame % 8]
            x0[t] = x1[(frame // 8) * 32 + role * 8 + frame % 8]
            return 0

        lax.fori_loop(0, 32, roll, 0)
        row = lax.broadcasted_iota(jnp.int32, (512, 1), 0)
        role, g = row // 128, (row % 128) // 16
        late = jnp.where(w * 8 + g >= 16 - offset, w, 0)
        far = jnp.where(role >= 2, 1, 0)
        low = (far * rowflag + (1 - far) * (1 - rowflag)) * at_row_end
        side_label = (role % 2) * at_col_end
        label = late * 4 + low * 2 + side_label
        for side in range(2):
            fq, fk = features(label, 120 * side)
            feat_q[side] = fq
            feat_k[side] = fk
        for chunk in (1, 0):
            attend(rolled, 0, chunk, feat_q, feat_k, mixed)
            out = project(1, x0[pl.ds(chunk * 16, 16)].reshape(256, D))
            second[pl.ds(w * 32 + chunk * 16, 16)] = out
            if chunk == 1:
                give_back(w, DIAG).start()
                give_back(w, VERT).start()
            else:
                give_back(w, RIGHT).start()
                keep(w).start()
        return 0

    lax.fori_loop(0, 2, block1, 0)

    for w in range(2):
        keep(w).wait()
        for role in (RIGHT, VERT, DIAG):
            exchange(w, role).wait_send()
            give_back(w, role).wait()
    for c in range(2):
        @pl.when(core == c)
        def _():
            for b in range(2):
                for copy, forward in zip(parts(c, b), relays(c, b)):
                    copy.wait_send()
                    forward.wait_send()


def finish_body(shift, y, out):
    step = pl.program_id(0)
    rowflag = shift[1]
    pick = quadrant_matrix(rowflag).astype(BF16)
    for f in range(4):
        g = (step * 4 + f - shift[0] + 16) % 16
        base = (g // 8) * 32 + g % 8
        rows = jnp.concatenate([y[base + role * 8] for role in range(4)], axis=0)
        x = lax.dot_general(pick, rows, (((0,), (0,)), ((), ())), preferred_element_type=F32)
        out[f] = x.reshape(8, 8, D).astype(BF16)


def local(latent, qkv_weight, proj_weight, modulation, regions, frame_shift):
    wa = lax.axis_index("wa")
    rowflag = 1 - wa % 2

    grid = regions.reshape(2, 8, 2, 4, 2, 4)
    flipped = jnp.where(rowflag == 1, grid, grid[:, :, ::-1])
    order = [(1, 1), (0, 0), (0, 1), (1, 0)]
    label = jnp.stack([flipped[:, :, i, :, j, :] for i, j in order], axis=1).reshape(1024, 1)
    lane = lax.broadcasted_iota(jnp.int32, (2, 1024, 128), 2)
    lane = lane - 120 * lax.broadcasted_iota(jnp.int32, (2, 1024, 128), 0)
    inside = jnp.logical_and(lane >= 0, lane < 8)
    same = lane == label[None]
    fq = jnp.where(jnp.logical_and(inside, same), 1.0, 0.0).astype(BF16)
    fk = jnp.where(jnp.logical_and(inside, jnp.logical_not(same)), -BIG, 0.0).astype(BF16)
    labels = jnp.stack([fq, fk])

    vmem = pl.BlockSpec(memory_space=pltpu.VMEM)
    anywhere = pl.BlockSpec(memory_space=pl.ANY)
    smem = pl.BlockSpec(memory_space=pltpu.SMEM)
    tiles = pltpu.VMEM((64, 16, D), BF16)
    dma = pltpu.SemaphoreType.DMA
    joined = pl.pallas_call(
        body,
        out_shape=jax.ShapeDtypeStruct((64, 16, D), BF16),
        in_specs=[vmem, anywhere, vmem, vmem, vmem, smem],
        out_specs=anywhere,
        scratch_shapes=[
            pltpu.VMEM((2, D, 3 * D), BF16),
            tiles, tiles, tiles,
            pltpu.VMEM((64, 16, 3 * D), BF16),
            pltpu.VMEM((32, 16, 3 * D), BF16),
            pltpu.VMEM((256, D), F32),
            tiles, tiles,
            pltpu.VMEM((2, 512, 128), BF16),
            pltpu.VMEM((2, 512, 128), BF16),
            pltpu.VMEM((2, D, HD), BF16),
            pltpu.VMEM((2, 8, 2 * HD, D), BF16),
            dma((2, 3)),
            dma, dma,
            dma((2, 7)), dma((2, 7)), dma((2, 7)), dma((2, 7)),
            dma((2, 3)), dma((2, 3)), dma((2, 3)), dma((2, 3)),
            dma((2,)),
        ],
        compiler_params=pltpu.CompilerParams(
            collective_id=0, has_side_effects=True, vmem_limit_bytes=62 << 20
        ),
        name="blocks",
    )(latent, qkv_weight, proj_weight, modulation, labels, frame_shift)

    numbers = jnp.stack([frame_shift[0], rowflag.astype(jnp.int32)])
    return pl.pallas_call(
        finish_body,
        out_shape=jax.ShapeDtypeStruct((16, 8, 8, D), BF16),
        grid_spec=pltpu.PrefetchScalarGridSpec(
            num_scalar_prefetch=1,
            grid=(4,),
            in_specs=[pl.BlockSpec((64, 16, D), lambda i, s: (0, 0, 0))],
            out_specs=pl.BlockSpec((4, 8, 8, D), lambda i, s: (i, 0, 0, 0)),
        ),
        compiler_params=pltpu.CompilerParams(vmem_limit_bytes=32 << 20),
        name="finish",
    )(numbers, joined)


def solution(mesh):
    in_specs = (P(None, "ha", "wa", None), P(), P(None, None, "wa"), P(), P(None, "ha", "wa"), P())
    out_specs = P(None, "ha", "wa", None)
    return jax.shard_map(local, mesh=mesh, in_specs=in_specs, out_specs=out_specs, check_vma=False)
```

```python
import functools
import math

import jax
import jax.numpy as jnp
from jax import lax
from jax.experimental import pallas as pl
from jax.experimental.pallas import tpu as pltpu
from jax.sharding import PartitionSpec as P

D = 1152
HEADS = 16
HD = 72
BIG = 1e30
SCALE = math.log2(math.e) / math.sqrt(HD)
F32 = jnp.float32
BF16 = jnp.bfloat16
MESH = pl.DeviceIdType.MESH
NT = (((1,), (1,)), ((), ()))

OWN, RIGHT, VERT, DIAG = range(4)


def quadrant_matrix(rowflag, leftflag):
    out = lax.broadcasted_iota(jnp.int32, (64, 64), 0)
    inn = lax.broadcasted_iota(jnp.int32, (64, 64), 1)
    role = out // 16
    half_j = 1 - role % 2
    flag = jnp.where(half_j == 1, rowflag, leftflag)
    half_i = jnp.where(role < 2, flag, 1 - flag)
    row = half_i * 4 + (out % 16) // 4
    col = half_j * 4 + out % 4
    return jnp.where(inn == row * 8 + col, 1.0, 0.0)


def head_span(h):
    start = (HD * h) // 128 * 128
    offset = HD * h - start
    return start, offset, (128 if offset + HD <= 128 else 256)


def lane_row(width, low, high):
    lane = lax.broadcasted_iota(jnp.int32, (1, width), 1)
    return jnp.where(jnp.logical_and(lane >= low, lane < high), 1.0, 0.0).astype(BF16)


def layer_scale(x, m0, m1):
    center = jnp.mean(x, -1, keepdims=True)
    moved = x - center
    spread = jnp.mean(moved * moved, -1, keepdims=True)
    return (moved * lax.rsqrt(spread + 1e-6) * (1.0 + m1) + m0).astype(BF16)


def features(label, rows):
    lane = lax.broadcasted_iota(jnp.int32, (rows, 128), 1)
    out = []
    for low in (0, 120):
        inside = jnp.logical_and(lane >= low, lane < low + 8)
        same = lane - low == label
        fq = jnp.where(jnp.logical_and(inside, same), 1.0, 0.0)
        fk = jnp.where(jnp.logical_and(inside, jnp.logical_not(same)), -BIG, 0.0)
        out.append((fq.astype(BF16), fk.astype(BF16)))
    return out


def attend(qkv, base, chunk, fq, fk, mixed):
    def scores(h):
        start, offset, width = head_span(h)
        side = 1 if offset == 0 else 0
        q = qkv[pl.ds(base + chunk * 16, 16), :, start : start + width].reshape(256, width)
        k = qkv[pl.ds(base, 32), :, D + start : D + start + width].reshape(512, width)
        mask = lane_row(width, offset, offset + HD)
        first = mask[:, :128]
        q0 = q[:, :128] * first + fq[side, pl.ds(base + chunk * 16, 16)].reshape(256, 128)
        k = k * mask
        k0 = k[:, :128] + fk[side, pl.ds(base, 32)].reshape(512, 128)
        if width == 256:
            q0 = jnp.concatenate([q0, q[:, 128:]], axis=1)
            k0 = jnp.concatenate([k0, k[:, 128:]], axis=1)
        return lax.dot_general(q0, k0, NT, preferred_element_type=F32)

    def values(h, s):
        start, offset, width = head_span(h)
        free = 127 if offset == 0 else 0
        s = s - jnp.max(s, axis=1, keepdims=True)
        weights = jnp.exp2(s).astype(BF16)
        v = qkv[pl.ds(base, 32), :, 2 * D + start : 2 * D + start + width].reshape(512, width)
        ones = lane_row(128, free, free + 1)
        v0 = v[:, :128] * (1.0 - ones) + ones
        if width == 256:
            v0 = jnp.concatenate([v0, v[:, 128:]], axis=1)
        out = jnp.dot(weights, v0, preferred_element_type=F32)
        out = out * (1.0 / out[:, free : free + 1])
        head = out[:, :128]
        if offset > 0:
            lane = lax.broadcasted_iota(jnp.int32, (256, 128), 1)
            head = jnp.where(lane >= offset, head, mixed[:, start : start + 128])
        mixed[:, start : start + 128] = head
        if width == 256:
            mixed[:, start + 128 : start + 256] = out[:, 128:]

    held = None
    for h in range(HEADS):
        s = scores(h)
        if held is not None:
            values(h - 1, held)
        held = s
    values(HEADS - 1, held)


def body(
    lat, weights, shard, mod, regions, shift,
    result,
    wbuf, x0, x1, scaled, qkv, rolled, mixed, first, second, back, final, feat_q, feat_k,
    mine, sib, pairs,
    load_sem, sib_send, sib_recv, x_send, x_recv, flip_send, flip_recv, rel_send, rel_recv,
    out_send, out_recv, back_send, back_recv, end_sem,
):
    ha, wa = lax.axis_index("ha"), lax.axis_index("wa")
    core = wa % 2
    ylo = (wa // 2) % 2
    xx = wa // 4
    chip = wa // 2
    rowflag = 1 - (core + ylo) % 2
    leftflag = core * (1 - rowflag) + (1 - core) * rowflag
    step = 2 * rowflag - 1
    leftstep = 2 * leftflag - 1

    def at(h, w):
        return ((h + 8) % 8, (w + 16) % 16)

    sibling = at(ha, wa + 1 - 2 * core)
    across = [
        ((ha + 4 * far) % 8, (xx * 2 + 1 - ylo) * 2 + core) for far in (core, 1)
    ]

    def along(k):
        x = (xx + k + 5) % 4
        return (ha, (x * 2 + ylo) * 2 + core), x * 2 + ylo

    send_to = {RIGHT: at(ha, wa - 1), VERT: at(ha - step, wa), DIAG: at(ha - leftstep, wa - 1)}
    back_to = {RIGHT: at(ha, wa + 1), VERT: at(ha + step, wa), DIAG: at(ha + step, wa + 1)}

    def loads(b):
        out = []
        for part in range(3):
            cols = pl.ds(part * D, D)
            out.append(
                pltpu.make_async_copy(weights.at[b, :, cols], wbuf.at[:, cols], load_sem.at[b, part])
            )
        return out

    for copy in loads(0):
        copy.start()

    barrier = pltpu.get_barrier_semaphore()
    greet = [sibling] + across + [along(k)[0] for k in range(3)]
    greet += list(send_to.values()) + list(back_to.values())
    for device in greet:
        pl.semaphore_signal(barrier, inc=1, device_id=device, device_id_type=MESH)
    pl.semaphore_wait(barrier, len(greet))

    def remote(src, dst, send, recv, device):
        return pltpu.make_async_remote_copy(
            src_ref=src, dst_ref=dst, send_sem=send, recv_sem=recv,
            device_id=device, device_id_type=MESH,
        )

    pad = jnp.zeros((8, D), F32)
    for b in range(2):
        mine[b] = jnp.concatenate([shard[b].astype(F32), pad], axis=0).astype(BF16)
    swap = remote(mine, sib, sib_send, sib_recv, sibling)
    swap.start()

    pick = quadrant_matrix(rowflag, leftflag).astype(BF16)
    places = jnp.dot(
        pick, regions[...].reshape(64, 16).astype(F32).astype(BF16), preferred_element_type=F32
    ).astype(jnp.int32)

    def prepare_frame(f):
        x = lat[f].astype(F32).reshape(64, D).astype(BF16)
        x = jnp.dot(pick, x, preferred_element_type=F32)
        y = layer_scale(x, mod[0, 0:1], mod[1, 0:1])
        x = x.astype(BF16)
        frame = lax.broadcasted_iota(jnp.int32, (64, 16), 1)
        label = jnp.sum(jnp.where(frame == f, places, 0), axis=1, keepdims=True)
        feats = features(label, 64)
        base = (f // 8) * 32 + f % 8
        for role in range(4):
            rows = slice(role * 16, role * 16 + 16)
            x0[base + role * 8] = x[rows]
            scaled[base + role * 8] = y[rows]
            for side in range(2):
                feat_q[side, base + role * 8] = feats[side][0][rows]
                feat_k[side, base + role * 8] = feats[side][1][rows]

    def prepare(i, _):
        prepare_frame(2 * i)
        prepare_frame(2 * i + 1)
        return 0

    lax.fori_loop(0, 3, prepare, 0)

    swap.wait()
    for b in range(2):
        own = mine[b].astype(F32)[:HD]
        theirs = sib[b].astype(F32)[:HD]
        low = jnp.where(core == 0, own, theirs)
        high = jnp.where(core == 0, theirs, own)
        pairs[b, chip] = jnp.concatenate([low, high], axis=0).astype(BF16)

    spans = ((0, 80), (80, 64))

    def x_copies(c, b):
        ref = pairs.at[b, chip, pl.ds(*spans[c])]
        return [
            remote(ref, ref, x_send.at[b, k], x_recv.at[b, k], along(k)[0]) for k in range(3)
        ]

    def row_chips(y):
        return [xx * 2 + y] + [((xx - k + 3) % 4) * 2 + y for k in range(3)]

    def flip_copies(c, b):
        out = []
        for k, source in enumerate(row_chips(ylo)):
            ref = pairs.at[b, source, pl.ds(*spans[c])]
            out.append(remote(ref, ref, flip_send.at[b, k], flip_recv.at[b, k], across[b]))
        return out

    def relay_copies(c, b):
        out = []
        for k, source in enumerate(row_chips(ylo)[1:] + row_chips(1 - ylo)):
            ref = pairs.at[b, source, pl.ds(*spans[c])]
            out.append(remote(ref, ref, rel_send.at[b, k], rel_recv.at[b, k], sibling))
        return out

    def by_core(act):
        for c in range(2):
            @pl.when(core == c)
            def _():
                act(c)

    def gather_start(b):
        def act(c):
            flip_copies(c, b)[0].start()
            for copy in x_copies(c, b):
                copy.start()
        by_core(act)

    def gather_turn(b):
        def act(c):
            flips, relays = flip_copies(c, b)[1:], relay_copies(c, b)[:3]
            for copy, flip, relay in zip(x_copies(c, b), flips, relays):
                copy.wait_recv()
                flip.start()
                relay.start()
        by_core(act)

    def gather_relay(b):
        def act(c):
            for flip, relay in zip(flip_copies(c, b), relay_copies(c, b)[3:]):
                flip.wait_recv()
                relay.start()
        by_core(act)

    def gather_end(b):
        def act(c):
            for relay in relay_copies(1 - c, b):
                relay.wait_recv()
        by_core(act)

    gather_start(0)
    lax.fori_loop(3, 8, prepare, 0)

    def triple(place, count, part):
        rows = scaled[place].reshape(count * 16, D)
        cols = pl.ds(pl.multiple_of(part * D, 128), D)
        out = jnp.dot(rows, wbuf[:, cols], preferred_element_type=F32)
        out = out * jnp.where(part == 0, SCALE, 1.0)
        qkv[place, :, cols] = out.astype(BF16).reshape(count, 16, D)

    def project(b, x, w):
        weight = pairs[b].reshape(D, D)
        branch = lax.dot_general(mixed[w].astype(BF16), weight, NT, preferred_element_type=F32)
        return (x.astype(F32) + mod[2, b : b + 1] * branch).astype(BF16).reshape(16, 16, D)

    for copy in loads(0):
        copy.wait()

    def make0(i, _):
        triple(pl.ds((i // 3) * 32, 32), 32, i % 3)
        return 0

    lax.fori_loop(0, 4, make0, 0)
    gather_turn(0)
    gather_start(1)
    lax.fori_loop(4, 6, make0, 0)
    for copy in loads(1):
        copy.start()

    def exchange(w, role):
        place = pl.ds(w * 32 + role * 8, 8)
        return remote(
            first.at[place], x1.at[place], out_send.at[w, role - 1], out_recv.at[w, role - 1],
            send_to[role],
        )

    def ahead(w, _):
        attend(qkv, w * 32, 1, feat_q, feat_k, mixed.at[w])

        @pl.when(w == 0)
        def _():
            gather_relay(0)
        return 0

    lax.fori_loop(0, 2, ahead, 0)
    gather_turn(1)
    gather_end(0)

    def far_pieces(w, _):
        here = pl.ds(w * 32 + 16, 16)
        first[here] = project(0, x0[here].reshape(256, D), w)
        exchange(w, DIAG).start()
        exchange(w, VERT).start()
        return 0

    lax.fori_loop(0, 2, far_pieces, 0)

    def near_pieces(w, _):
        base = w * 32
        attend(qkv, base, 0, feat_q, feat_k, mixed.at[w])
        out = project(0, x0[pl.ds(base, 16)].reshape(256, D), w)
        x1[pl.ds(base, 8)] = out[:8]
        first[pl.ds(base + 8, 8)] = out[8:]
        exchange(w, RIGHT).start()
        return 0

    lax.fori_loop(0, 2, near_pieces, 0)

    offset = shift[0]
    row_block = (ha + rowflag + 7) % 8
    at_row_end = jnp.where(row_block == 7, 1, 0)
    at_col_end = jnp.where(wa == 15, 1, 0)

    def label_tiles(i, _):
        w, role = i // 4, i % 4
        frame = w * 8 + lax.broadcasted_iota(jnp.int32, (128, 1), 0) // 16
        late = jnp.where(frame >= 16 - offset, w, 0)
        far = role // 2
        low = (far * rowflag + (1 - far) * (1 - rowflag)) * at_row_end
        feats = features(late * 4 + low * 2 + (role % 2) * at_col_end, 128)
        for side in range(2):
            feat_q[side, pl.ds(i * 8, 8)] = feats[side][0].reshape(8, 16, 128)
            feat_k[side, pl.ds(i * 8, 8)] = feats[side][1].reshape(8, 16, 128)
        return 0

    lax.fori_loop(0, 8, label_tiles, 0)

    for copy in loads(1):
        copy.wait()

    def norm(t, _):
        for k in range(2):
            place = pl.ds(t * 8 + k * 4, 4)
            x = x1[place].reshape(64, D).astype(F32)
            scaled[place] = layer_scale(x, mod[0, 1:2], mod[1, 1:2]).reshape(4, 16, D)
        return 0

    for chunk in (1, 0):
        def make1(w, _):
            for role in ((VERT, DIAG) if chunk == 1 else (RIGHT,)):
                exchange(w, role).wait_recv()
            start = w * 32 + chunk * 16
            lax.fori_loop(start // 8, start // 8 + 2, norm, 0)

            def part(p, _):
                triple(pl.ds(start, 16), 16, p)
                return 0

            lax.fori_loop(0, 3, part, 0)
            return 0

        lax.fori_loop(0, 2, make1, 0)
        if chunk == 1:
            gather_relay(1)

    def give_back(w, role):
        place = pl.ds(w * 32 + role * 8, 8)
        return remote(
            second.at[place], back.at[place], back_send.at[w, role - 1],
            back_recv.at[w, role - 1], back_to[role],
        )

    def roll(i, _):
        w, role = i // 4, i % 4
        for g in range(8):
            frame = (w * 8 + g + offset) % 16
            source = (frame // 8) * 32 + role * 8 + frame % 8
            rolled[i * 8 + g] = qkv[source]
            x0[i * 8 + g] = x1[source]
        return 0

    lax.fori_loop(0, 8, roll, 0)

    for chunk in (1, 0):
        def block1(w, _):
            base = w * 32
            attend(rolled, base, chunk, feat_q, feat_k, mixed.at[w])
            here = pl.ds(base + chunk * 16, 16)
            if chunk == 1:
                @pl.when(w == 0)
                def _():
                    gather_end(1)
            second[here] = project(1, x0[here].reshape(256, D), w)
            if chunk == 1:
                give_back(w, DIAG).start()
                give_back(w, VERT).start()
            else:
                give_back(w, RIGHT).start()
            return 0

        lax.fori_loop(0, 2, block1, 0)

    for w in range(2):
        for role in (RIGHT, VERT, DIAG):
            give_back(w, role).wait_recv()

    def last(i):
        return pltpu.make_async_copy(
            final.at[pl.ds(i * 4, 4)], result.at[pl.ds(i * 4, 4)], end_sem.at[i]
        )

    def restore(i, _):
        for k in range(4):
            g = (i * 4 + k - offset + 16) % 16
            base = (g // 8) * 32 + g % 8
            rows = [second[base]] + [back[base + role * 8] for role in (RIGHT, VERT, DIAG)]
            x = lax.dot_general(
                pick, jnp.concatenate(rows, axis=0), (((0,), (0,)), ((), ())),
                preferred_element_type=F32,
            )
            final[i * 4 + k] = x.reshape(8, 8, D).astype(BF16)
        last(i).start()
        return 0

    lax.fori_loop(0, 4, restore, 0)

    for w in range(2):
        for role in (RIGHT, VERT, DIAG):
            exchange(w, role).wait_send()
            give_back(w, role).wait_send()

    def act(c):
        for b in range(2):
            for copy in x_copies(c, b) + flip_copies(c, b) + relay_copies(c, b):
                copy.wait_send()

    by_core(act)
    for i in range(4):
        last(i).wait()


def local(latent, qkv_weight, proj_weight, modulation, regions, frame_shift):
    vmem = pl.BlockSpec(memory_space=pltpu.VMEM)
    anywhere = pl.BlockSpec(memory_space=pl.ANY)
    smem = pl.BlockSpec(memory_space=pltpu.SMEM)
    tiles = pltpu.VMEM((64, 16, D), BF16)
    triples = pltpu.VMEM((64, 16, 3 * D), BF16)
    feats = pltpu.VMEM((2, 64, 16, 128), BF16)
    shards = pltpu.VMEM((2, 80, D), BF16)
    dma = pltpu.SemaphoreType.DMA
    return pl.pallas_call(
        body,
        out_shape=jax.ShapeDtypeStruct((16, 8, 8, D), BF16),
        in_specs=[vmem, anywhere, vmem, vmem, vmem, smem],
        out_specs=anywhere,
        scratch_shapes=[
            pltpu.VMEM((D, 3 * D), BF16),
            tiles, tiles, tiles,
            triples, triples,
            pltpu.VMEM((2, 256, D), F32),
            tiles, tiles, tiles,
            pltpu.VMEM((16, 8, 8, D), BF16),
            feats, feats,
            shards, shards,
            pltpu.VMEM((2, 8, 2 * HD, D), BF16),
            dma((2, 3)),
            dma, dma,
            dma((2, 3)), dma((2, 3)), dma((2, 4)), dma((2, 4)), dma((2, 7)), dma((2, 7)),
            dma((2, 3)), dma((2, 3)), dma((2, 3)), dma((2, 3)),
            dma((4,)),
        ],
        compiler_params=pltpu.CompilerParams(
            collective_id=0, has_side_effects=True, vmem_limit_bytes=62 << 20
        ),
        name="blocks",
    )(
        latent,
        qkv_weight,
        jnp.swapaxes(proj_weight, 1, 2),
        jnp.swapaxes(modulation, 0, 1),
        jnp.transpose(regions, (1, 2, 0)),
        frame_shift,
    )


def solution(mesh):
    in_specs = (P(None, "ha", "wa", None), P(), P(None, None, "wa"), P(), P(None, "ha", "wa"), P())
    out_specs = P(None, "ha", "wa", None)
    return jax.shard_map(local, mesh=mesh, in_specs=in_specs, out_specs=out_specs, check_vma=False)
```

```python
import functools
import math

import jax
import jax.numpy as jnp
from jax import lax
from jax.experimental import pallas as pl
from jax.experimental.pallas import tpu as pltpu
from jax.sharding import PartitionSpec as P

D = 1152
HEADS = 16
HD = 72
BIG = 1e30
SCALE = math.log2(math.e) / math.sqrt(HD)
F32 = jnp.float32
BF16 = jnp.bfloat16
MESH = pl.DeviceIdType.MESH
NT = (((1,), (1,)), ((), ()))

OWN, RIGHT, VERT, DIAG = range(4)


def corner_flags(wa):
    core, ylo = wa % 2, (wa // 2) % 2
    rowflag = 1 - (core + ylo) % 2
    return rowflag, core * (1 - rowflag) + (1 - core) * rowflag


def quadrant_matrix(rowflag, leftflag):
    out = lax.broadcasted_iota(jnp.int32, (64, 64), 0)
    inn = lax.broadcasted_iota(jnp.int32, (64, 64), 1)
    role = out // 16
    half_j = 1 - role % 2
    flag = jnp.where(half_j == 1, rowflag, leftflag)
    half_i = jnp.where(role < 2, flag, 1 - flag)
    row = half_i * 4 + (out % 16) // 4
    col = half_j * 4 + out % 4
    return jnp.where(inn == row * 8 + col, 1.0, 0.0)


def head_span(h):
    start = (HD * h) // 128 * 128
    offset = HD * h - start
    return start, offset, (128 if offset + HD <= 128 else 256)


def lane_row(width, low, high):
    lane = lax.broadcasted_iota(jnp.int32, (1, width), 1)
    return jnp.where(jnp.logical_and(lane >= low, lane < high), 1.0, 0.0).astype(BF16)


def layer_scale(x, m0, m1):
    center = jnp.mean(x, -1, keepdims=True)
    moved = x - center
    spread = jnp.mean(moved * moved, -1, keepdims=True)
    return (moved * lax.rsqrt(spread + 1e-6) * (1.0 + m1) + m0).astype(BF16)


def features(label, rows):
    lane = lax.broadcasted_iota(jnp.int32, (rows, 128), 1)
    out = []
    for low in (0, 120):
        inside = jnp.logical_and(lane >= low, lane < low + 8)
        same = lane - low == label
        fq = jnp.where(jnp.logical_and(inside, same), 1.0, 0.0)
        fk = jnp.where(jnp.logical_and(inside, jnp.logical_not(same)), -BIG, 0.0)
        out.append((fq.astype(BF16), fk.astype(BF16)))
    return out


def attend(qkv, base, chunk, fq, fk, mixed):
    def scores(h):
        start, offset, width = head_span(h)
        side = 1 if offset == 0 else 0
        q = qkv[pl.ds(base + chunk * 16, 16), :, start : start + width].reshape(256, width)
        k = qkv[pl.ds(base, 32), :, D + start : D + start + width].reshape(512, width)
        mask = lane_row(width, offset, offset + HD)
        first = mask[:, :128]
        q0 = q[:, :128] * first + fq[side, pl.ds(base + chunk * 16, 16)].reshape(256, 128)
        k = k * mask
        k0 = k[:, :128] + fk[side, pl.ds(base, 32)].reshape(512, 128)
        if width == 256:
            q0 = jnp.concatenate([q0, q[:, 128:]], axis=1)
            k0 = jnp.concatenate([k0, k[:, 128:]], axis=1)
        return lax.dot_general(q0, k0, NT, preferred_element_type=F32)

    def values(h, s):
        start, offset, width = head_span(h)
        free = 127 if offset == 0 else 0
        s = s - jnp.max(s, axis=1, keepdims=True)
        weights = jnp.exp2(s).astype(BF16)
        v = qkv[pl.ds(base, 32), :, 2 * D + start : 2 * D + start + width].reshape(512, width)
        ones = lane_row(128, free, free + 1)
        v0 = v[:, :128] * (1.0 - ones) + ones
        if width == 256:
            v0 = jnp.concatenate([v0, v[:, 128:]], axis=1)
        out = jnp.dot(weights, v0, preferred_element_type=F32)
        out = out * (1.0 / out[:, free : free + 1])
        head = out[:, :128]
        if offset > 0:
            lane = lax.broadcasted_iota(jnp.int32, (256, 128), 1)
            head = jnp.where(lane >= offset, head, mixed[:, start : start + 128])
        mixed[:, start : start + 128] = head
        if width == 256:
            mixed[:, start + 128 : start + 256] = out[:, 128:]

    held = None
    for h in range(HEADS):
        s = scores(h)
        if held is not None:
            values(h - 1, held)
        held = s
    values(HEADS - 1, held)


def body(
    lat, weights, shard, mod, regions, shift,
    result,
    wbuf, x0, x1, scaled, qkv, rolled, mixed, first, second, passed, feat_q, feat_k,
    mine, sib, pairs,
    load_sem, sib_send, sib_recv, x_send, x_recv, flip_send, flip_recv, rel_send, rel_recv,
    out_send, out_recv, back_send, back_recv, pass_send, pass_recv, own_sem,
):
    ha, wa = lax.axis_index("ha"), lax.axis_index("wa")
    core = wa % 2
    ylo = (wa // 2) % 2
    xx = wa // 4
    chip = wa // 2
    depth = ha % 4
    rowflag, leftflag = corner_flags(wa)
    step = 2 * rowflag - 1
    leftstep = 2 * leftflag - 1

    def at(h, w):
        return ((h + 8) % 8, (w + 16) % 16)

    sibling = at(ha, wa + 1 - 2 * core)
    across = [
        ((ha + 4 * far) % 8, (xx * 2 + 1 - ylo) * 2 + core) for far in (core, 1)
    ]

    def along(k):
        x = (xx + k + 5) % 4
        return (ha, (x * 2 + ylo) * 2 + core), x * 2 + ylo

    send_to = {RIGHT: at(ha, wa - 1), VERT: at(ha - step, wa), DIAG: at(ha - leftstep, wa - 1)}
    back_to = {RIGHT: at(ha, wa + 1), VERT: at(ha + step, wa), DIAG: at(ha + step, wa + 1)}

    def loads(b):
        out = []
        for part in range(3):
            cols = pl.ds(part * D, D)
            out.append(
                pltpu.make_async_copy(weights.at[b, :, cols], wbuf.at[:, cols], load_sem.at[b, part])
            )
        return out

    for copy in loads(0):
        copy.start()

    barrier = pltpu.get_barrier_semaphore()
    greet = [sibling] + across + [along(k)[0] for k in range(3)]
    greet += list(send_to.values()) + list(back_to.values())
    for device in greet:
        pl.semaphore_signal(barrier, inc=1, device_id=device, device_id_type=MESH)
    pl.semaphore_wait(barrier, len(greet))

    def remote(src, dst, send, recv, device):
        return pltpu.make_async_remote_copy(
            src_ref=src, dst_ref=dst, send_sem=send, recv_sem=recv,
            device_id=device, device_id_type=MESH,
        )

    pad = jnp.zeros((8, D), F32)
    for b in range(2):
        mine[b] = jnp.concatenate([shard[b].astype(F32), pad], axis=0).astype(BF16)
    swap = remote(mine, sib, sib_send, sib_recv, sibling)
    swap.start()

    pick = quadrant_matrix(rowflag, leftflag).astype(BF16)
    places = jnp.dot(
        pick, regions[...].reshape(64, 16).astype(F32).astype(BF16), preferred_element_type=F32
    ).astype(jnp.int32)

    def prepare_frame(f):
        x = lat[f].astype(F32).reshape(64, D).astype(BF16)
        x = jnp.dot(pick, x, preferred_element_type=F32)
        y = layer_scale(x, mod[0, 0:1], mod[1, 0:1])
        x = x.astype(BF16)
        frame = lax.broadcasted_iota(jnp.int32, (64, 16), 1)
        label = jnp.sum(jnp.where(frame == f, places, 0), axis=1, keepdims=True)
        feats = features(label, 64)
        base = (f // 8) * 32 + f % 8
        for role in range(4):
            rows = slice(role * 16, role * 16 + 16)
            x0[base + role * 8] = x[rows]
            scaled[base + role * 8] = y[rows]
            for side in range(2):
                feat_q[side, base + role * 8] = feats[side][0][rows]
                feat_k[side, base + role * 8] = feats[side][1][rows]

    def prepare(i, _):
        prepare_frame(2 * i)
        prepare_frame(2 * i + 1)
        return 0

    lax.fori_loop(0, 3, prepare, 0)

    swap.wait()
    for b in range(2):
        own = mine[b].astype(F32)[:HD]
        theirs = sib[b].astype(F32)[:HD]
        low = jnp.where(core == 0, own, theirs)
        high = jnp.where(core == 0, theirs, own)
        pairs[b, chip] = jnp.concatenate([low, high], axis=0).astype(BF16)

    spans = ((0, 80), (80, 64))

    def x_copies(c, b):
        ref = pairs.at[b, chip, pl.ds(*spans[c])]
        return [
            remote(ref, ref, x_send.at[b, k], x_recv.at[b, k], along(k)[0]) for k in range(3)
        ]

    def row_chips(y):
        return [xx * 2 + y] + [((xx - k + 3) % 4) * 2 + y for k in range(3)]

    def flip_copies(c, b):
        out = []
        for k, source in enumerate(row_chips(ylo)):
            ref = pairs.at[b, source, pl.ds(*spans[c])]
            out.append(remote(ref, ref, flip_send.at[b, k], flip_recv.at[b, k], across[b]))
        return out

    def relay_copies(c, b):
        out = []
        for k, source in enumerate(row_chips(ylo)[1:] + row_chips(1 - ylo)):
            ref = pairs.at[b, source, pl.ds(*spans[c])]
            out.append(remote(ref, ref, rel_send.at[b, k], rel_recv.at[b, k], sibling))
        return out

    def by_core(act):
        for c in range(2):
            @pl.when(core == c)
            def _():
                act(c)

    def gather_start(b):
        def act(c):
            flip_copies(c, b)[0].start()
            for copy in x_copies(c, b):
                copy.start()
        by_core(act)

    def gather_turn(b):
        def act(c):
            flips, relays = flip_copies(c, b)[1:], relay_copies(c, b)[:3]
            for copy, flip, relay in zip(x_copies(c, b), flips, relays):
                copy.wait_recv()
                flip.start()
                relay.start()
        by_core(act)

    def gather_relay(b):
        def act(c):
            for flip, relay in zip(flip_copies(c, b), relay_copies(c, b)[3:]):
                flip.wait_recv()
                relay.start()
        by_core(act)

    def gather_end(b):
        def act(c):
            for relay in relay_copies(1 - c, b):
                relay.wait_recv()
        by_core(act)

    gather_start(0)
    lax.fori_loop(3, 8, prepare, 0)

    def triple(place, count, part):
        rows = scaled[place].reshape(count * 16, D)
        cols = pl.ds(pl.multiple_of(part * D, 128), D)
        out = jnp.dot(rows, wbuf[:, cols], preferred_element_type=F32)
        out = out * jnp.where(part == 0, SCALE, 1.0)
        qkv[place, :, cols] = out.astype(BF16).reshape(count, 16, D)

    def project(b, x, w):
        weight = pairs[b].reshape(D, D)
        branch = lax.dot_general(mixed[w].astype(BF16), weight, NT, preferred_element_type=F32)
        return (x.astype(F32) + mod[2, b : b + 1] * branch).astype(BF16).reshape(16, 16, D)

    for copy in loads(0):
        copy.wait()

    def make0(i, _):
        triple(pl.ds((i // 3) * 32, 32), 32, i % 3)
        return 0

    lax.fori_loop(0, 4, make0, 0)
    gather_turn(0)
    gather_start(1)
    lax.fori_loop(4, 6, make0, 0)
    for copy in loads(1):
        copy.start()

    def exchange(w, role):
        place = pl.ds(w * 32 + role * 8, 8)
        return remote(
            first.at[place], x1.at[place], out_send.at[w, role - 1], out_recv.at[w, role - 1],
            send_to[role],
        )

    def ahead(w, _):
        attend(qkv, w * 32, 1, feat_q, feat_k, mixed.at[w])

        @pl.when(w == 0)
        def _():
            gather_relay(0)
        return 0

    lax.fori_loop(0, 2, ahead, 0)
    gather_turn(1)
    gather_end(0)

    def far_pieces(w, _):
        here = pl.ds(w * 32 + 16, 16)
        first[here] = project(0, x0[here].reshape(256, D), w)
        exchange(w, DIAG).start()
        exchange(w, VERT).start()
        return 0

    lax.fori_loop(0, 2, far_pieces, 0)

    def near_pieces(w, _):
        base = w * 32
        attend(qkv, base, 0, feat_q, feat_k, mixed.at[w])
        out = project(0, x0[pl.ds(base, 16)].reshape(256, D), w)
        x1[pl.ds(base, 8)] = out[:8]
        first[pl.ds(base + 8, 8)] = out[8:]
        exchange(w, RIGHT).start()
        return 0

    lax.fori_loop(0, 2, near_pieces, 0)

    offset = shift[0]
    row_block = (ha + rowflag + 7) % 8
    at_row_end = jnp.where(row_block == 7, 1, 0)
    at_col_end = jnp.where(wa == 15, 1, 0)

    def label_tiles(i, _):
        w, role = i // 4, i % 4
        frame = w * 8 + lax.broadcasted_iota(jnp.int32, (128, 1), 0) // 16
        late = jnp.where(frame >= 16 - offset, w, 0)
        far = role // 2
        low = (far * rowflag + (1 - far) * (1 - rowflag)) * at_row_end
        feats = features(late * 4 + low * 2 + (role % 2) * at_col_end, 128)
        for side in range(2):
            feat_q[side, pl.ds(i * 8, 8)] = feats[side][0].reshape(8, 16, 128)
            feat_k[side, pl.ds(i * 8, 8)] = feats[side][1].reshape(8, 16, 128)
        return 0

    lax.fori_loop(0, 8, label_tiles, 0)

    for copy in loads(1):
        copy.wait()

    def norm(t, _):
        for k in range(2):
            place = pl.ds(t * 8 + k * 4, 4)
            x = x1[place].reshape(64, D).astype(F32)
            scaled[place] = layer_scale(x, mod[0, 1:2], mod[1, 1:2]).reshape(4, 16, D)
        return 0

    for chunk in (0, 1):
        def make1(w, _):
            for role in ((VERT, DIAG) if chunk == 1 else (RIGHT,)):
                exchange(w, role).wait_recv()
            start = w * 32 + chunk * 16
            lax.fori_loop(start // 8, start // 8 + 2, norm, 0)

            def part(p, _):
                triple(pl.ds(start, 16), 16, p)
                return 0

            lax.fori_loop(0, 3, part, 0)
            return 0

        lax.fori_loop(0, 2, make1, 0)
        if chunk == 0:
            gather_relay(1)

    by_z = core * jnp.where(depth == 3, 1 - rowflag, jnp.where(depth == 0, rowflag, 0))
    passes = core * jnp.where(depth == 2, 1 - rowflag, jnp.where(depth == 1, rowflag, 0))

    def give_back(w, role):
        place = pl.ds(w * 32 + role * 8, 8)
        return remote(
            second.at[place], result.at[place], back_send.at[w, role - 1],
            back_recv.at[w, role - 1], back_to[role],
        )

    def by_neighbour(w):
        place = pl.ds(w * 32 + DIAG * 8, 8)
        return remote(
            second.at[place], passed.at[w], pass_send.at[w], pass_recv.at[w], back_to[VERT]
        )

    def pass_back(w):
        place = pl.ds(w * 32 + DIAG * 8, 8)
        return remote(
            passed.at[w], result.at[place], pass_send.at[w], back_recv.at[w, DIAG - 1],
            back_to[RIGHT],
        )

    def keep(w):
        place = pl.ds(w * 32, 8)
        return pltpu.make_async_copy(second.at[place], result.at[place], own_sem.at[w])

    def roll(i, _):
        w, role = i // 4, i % 4
        for g in range(8):
            frame = (w * 8 + g + offset) % 16
            source = (frame // 8) * 32 + role * 8 + frame % 8
            rolled[i * 8 + g] = qkv[source]
            x0[i * 8 + g] = x1[source]
        return 0

    lax.fori_loop(0, 8, roll, 0)

    for chunk in (1, 0):
        def block1(w, _):
            base = w * 32
            attend(rolled, base, chunk, feat_q, feat_k, mixed.at[w])
            here = pl.ds(base + chunk * 16, 16)
            if chunk == 1:
                @pl.when(w == 0)
                def _():
                    gather_end(1)
            second[here] = project(1, x0[here].reshape(256, D), w)
            if chunk == 1:
                give_back(w, VERT).start()

                @pl.when(by_z == 1)
                def _():
                    by_neighbour(w).start()

                @pl.when(by_z == 0)
                def _():
                    give_back(w, DIAG).start()
            else:
                give_back(w, RIGHT).start()
                keep(w).start()
            return 0

        lax.fori_loop(0, 2, block1, 0)

    @pl.when(passes == 1)
    def _():
        for w in range(2):
            by_neighbour(w).wait_recv()
            pass_back(w).start()
        for w in range(2):
            pass_back(w).wait_send()

    for w in range(2):
        keep(w).wait()
        for role in (RIGHT, VERT, DIAG):
            exchange(w, role).wait_send()
            give_back(w, role).wait_recv()
        for role in (RIGHT, VERT):
            give_back(w, role).wait_send()

        @pl.when(by_z == 1)
        def _():
            by_neighbour(w).wait_send()

        @pl.when(by_z == 0)
        def _():
            give_back(w, DIAG).wait_send()

    def act(c):
        for b in range(2):
            for copy in x_copies(c, b) + flip_copies(c, b) + relay_copies(c, b):
                copy.wait_send()

    by_core(act)


def finish_body(shift, joined, out, tiles, final, in_sem, out_sem):
    back = quadrant_matrix(*corner_flags(lax.axis_index("wa"))).T.astype(BF16)

    def load(w, role):
        place = pl.ds(w * 32 + role * 8, 8)
        return pltpu.make_async_copy(joined.at[place], tiles.at[place], in_sem.at[w, role])

    for w in range(2):
        for role in range(4):
            load(w, role).start()

    def store(t):
        frame = (t + shift[0]) % 16
        return pltpu.make_async_copy(final.at[t], out.at[frame], out_sem.at[t])

    for w in range(2):
        for role in range(4):
            load(w, role).wait()

        for t in range(w * 8, w * 8 + 8):
            base = w * 32 + t % 8
            rows = jnp.concatenate([tiles[base + role * 8] for role in range(4)], axis=0)
            x = jnp.dot(back, rows, preferred_element_type=F32)
            final[t] = x.reshape(8, 8, D).astype(BF16)
            store(t).start()

    for t in range(16):
        store(t).wait()


def local(latent, qkv_weight, proj_weight, modulation, regions, frame_shift):
    vmem = pl.BlockSpec(memory_space=pltpu.VMEM)
    anywhere = pl.BlockSpec(memory_space=pl.ANY)
    smem = pl.BlockSpec(memory_space=pltpu.SMEM)
    tiles = pltpu.VMEM((64, 16, D), BF16)
    triples = pltpu.VMEM((64, 16, 3 * D), BF16)
    feats = pltpu.VMEM((2, 64, 16, 128), BF16)
    shards = pltpu.VMEM((2, 80, D), BF16)
    dma = pltpu.SemaphoreType.DMA
    joined = pl.pallas_call(
        body,
        out_shape=jax.ShapeDtypeStruct((64, 16, D), BF16),
        in_specs=[vmem, anywhere, vmem, vmem, vmem, smem],
        out_specs=anywhere,
        scratch_shapes=[
            pltpu.VMEM((D, 3 * D), BF16),
            tiles, tiles, tiles,
            triples, triples,
            pltpu.VMEM((2, 256, D), F32),
            tiles, tiles,
            pltpu.VMEM((2, 8, 16, D), BF16),
            feats, feats,
            shards, shards,
            pltpu.VMEM((2, 8, 2 * HD, D), BF16),
            dma((2, 3)),
            dma, dma,
            dma((2, 3)), dma((2, 3)), dma((2, 4)), dma((2, 4)), dma((2, 7)), dma((2, 7)),
            dma((2, 3)), dma((2, 3)), dma((2, 3)), dma((2, 3)),
            dma((2,)), dma((2,)), dma((2,)),
        ],
        compiler_params=pltpu.CompilerParams(
            collective_id=0, has_side_effects=True, vmem_limit_bytes=62 << 20
        ),
        name="blocks",
    )(
        latent,
        qkv_weight,
        jnp.swapaxes(proj_weight, 1, 2),
        jnp.swapaxes(modulation, 0, 1),
        jnp.transpose(regions, (1, 2, 0)),
        frame_shift,
    )
    return pl.pallas_call(
        finish_body,
        out_shape=jax.ShapeDtypeStruct((16, 8, 8, D), BF16),
        in_specs=[smem, anywhere],
        out_specs=anywhere,
        scratch_shapes=[tiles, pltpu.VMEM((16, 8, 8, D), BF16), dma((2, 4)), dma((16,))],
        compiler_params=pltpu.CompilerParams(vmem_limit_bytes=62 << 20),
        name="finish",
    )(frame_shift, joined)


def solution(mesh):
    in_specs = (P(None, "ha", "wa", None), P(), P(None, None, "wa"), P(), P(None, "ha", "wa"), P())
    out_specs = P(None, "ha", "wa", None)
    return jax.shard_map(local, mesh=mesh, in_specs=in_specs, out_specs=out_specs, check_vma=False)
```

```python
import functools
import math

import jax
import jax.numpy as jnp
from jax import lax
from jax.experimental import pallas as pl
from jax.experimental.pallas import tpu as pltpu
from jax.sharding import PartitionSpec as P

D = 1152
HEADS = 16
HD = 72
BIG = 1e30
SCALE = math.log2(math.e) / math.sqrt(HD)
F32 = jnp.float32
BF16 = jnp.bfloat16
MESH = pl.DeviceIdType.MESH
NT = (((1,), (1,)), ((), ()))

OWN, RIGHT, VERT, DIAG = range(4)


def corner_flags(wa):
    core, ylo = wa % 2, (wa // 2) % 2
    rowflag = 1 - (core + ylo) % 2
    return rowflag, core * (1 - rowflag) + (1 - core) * rowflag


def quadrant_matrix(rowflag, leftflag):
    out = lax.broadcasted_iota(jnp.int32, (64, 64), 0)
    inn = lax.broadcasted_iota(jnp.int32, (64, 64), 1)
    role = out // 16
    half_j = 1 - role % 2
    flag = jnp.where(half_j == 1, rowflag, leftflag)
    half_i = jnp.where(role < 2, flag, 1 - flag)
    row = half_i * 4 + (out % 16) // 4
    col = half_j * 4 + out % 4
    return jnp.where(inn == row * 8 + col, 1.0, 0.0)


def head_span(h):
    start = (HD * h) // 128 * 128
    offset = HD * h - start
    return start, offset, (128 if offset + HD <= 128 else 256)


def lane_row(width, low, high):
    lane = lax.broadcasted_iota(jnp.int32, (1, width), 1)
    return jnp.where(jnp.logical_and(lane >= low, lane < high), 1.0, 0.0).astype(BF16)


def layer_scale(x, m0, m1):
    center = jnp.mean(x, -1, keepdims=True)
    moved = x - center
    spread = jnp.mean(moved * moved, -1, keepdims=True)
    return (moved * lax.rsqrt(spread + 1e-6) * (1.0 + m1) + m0).astype(BF16)


def features(label, rows):
    lane = lax.broadcasted_iota(jnp.int32, (rows, 128), 1)
    out = []
    for low in (0, 120):
        inside = jnp.logical_and(lane >= low, lane < low + 8)
        same = lane - low == label
        fq = jnp.where(jnp.logical_and(inside, same), 1.0, 0.0)
        fk = jnp.where(jnp.logical_and(inside, jnp.logical_not(same)), -BIG, 0.0)
        out.append((fq.astype(BF16), fk.astype(BF16)))
    return out


def attend(qkv, base, chunk, fq, fk, mixed):
    def scores(h):
        start, offset, width = head_span(h)
        side = 1 if offset == 0 else 0
        q = qkv[pl.ds(base + chunk * 16, 16), :, start : start + width].reshape(256, width)
        k = qkv[pl.ds(base, 32), :, D + start : D + start + width].reshape(512, width)
        mask = lane_row(width, offset, offset + HD)
        first = mask[:, :128]
        q0 = q[:, :128] * first + fq[side, pl.ds(base + chunk * 16, 16)].reshape(256, 128)
        k = k * mask
        k0 = k[:, :128] + fk[side, pl.ds(base, 32)].reshape(512, 128)
        if width == 256:
            q0 = jnp.concatenate([q0, q[:, 128:]], axis=1)
            k0 = jnp.concatenate([k0, k[:, 128:]], axis=1)
        return lax.dot_general(q0, k0, NT, preferred_element_type=F32)

    def values(h, s):
        start, offset, width = head_span(h)
        free = 127 if offset == 0 else 0
        s = s - jnp.max(s, axis=1, keepdims=True)
        weights = jnp.exp2(s).astype(BF16)
        v = qkv[pl.ds(base, 32), :, 2 * D + start : 2 * D + start + width].reshape(512, width)
        ones = lane_row(128, free, free + 1)
        v0 = v[:, :128] * (1.0 - ones) + ones
        if width == 256:
            v0 = jnp.concatenate([v0, v[:, 128:]], axis=1)
        out = jnp.dot(weights, v0, preferred_element_type=F32)
        out = out * (1.0 / out[:, free : free + 1])
        head = out[:, :128]
        if offset > 0:
            lane = lax.broadcasted_iota(jnp.int32, (256, 128), 1)
            head = jnp.where(lane >= offset, head, mixed[:, start : start + 128])
        mixed[:, start : start + 128] = head
        if width == 256:
            mixed[:, start + 128 : start + 256] = out[:, 128:]

    held = [scores(0), scores(1)]
    for h in range(HEADS):
        if h + 2 < HEADS:
            held.append(scores(h + 2))
        values(h, held.pop(0))


def body(
    lat, weights, shard, mod, regions, shift,
    result,
    wbuf, x0, x1, scaled, qkv, rolled, mixed, first, second, passed, feat_q, feat_k,
    mine, sib, pairs,
    load_sem, sib_send, sib_recv, x_send, x_recv, flip_send, flip_recv, rel_send, rel_recv,
    out_send, out_recv, back_send, back_recv, pass_send, pass_recv, own_sem,
):
    ha, wa = lax.axis_index("ha"), lax.axis_index("wa")
    core = wa % 2
    ylo = (wa // 2) % 2
    xx = wa // 4
    chip = wa // 2
    depth = ha % 4
    rowflag, leftflag = corner_flags(wa)
    step = 2 * rowflag - 1
    leftstep = 2 * leftflag - 1

    def at(h, w):
        return ((h + 8) % 8, (w + 16) % 16)

    sibling = at(ha, wa + 1 - 2 * core)
    across = [
        ((ha + 4 * far) % 8, (xx * 2 + 1 - ylo) * 2 + core) for far in (core, 1)
    ]

    def along(k):
        x = (xx + k + 5) % 4
        return (ha, (x * 2 + ylo) * 2 + core), x * 2 + ylo

    send_to = {RIGHT: at(ha, wa - 1), VERT: at(ha - step, wa), DIAG: at(ha - leftstep, wa - 1)}
    back_to = {RIGHT: at(ha, wa + 1), VERT: at(ha + step, wa), DIAG: at(ha + step, wa + 1)}

    def loads(b):
        out = []
        for part in range(3):
            cols = pl.ds(part * D, D)
            out.append(
                pltpu.make_async_copy(weights.at[b, :, cols], wbuf.at[:, cols], load_sem.at[b, part])
            )
        return out

    for copy in loads(0):
        copy.start()

    barrier = pltpu.get_barrier_semaphore()
    greet = [sibling] + across + [along(k)[0] for k in range(3)]
    greet += list(send_to.values()) + list(back_to.values())
    for device in greet:
        pl.semaphore_signal(barrier, inc=1, device_id=device, device_id_type=MESH)
    pl.semaphore_wait(barrier, len(greet))

    def remote(src, dst, send, recv, device):
        return pltpu.make_async_remote_copy(
            src_ref=src, dst_ref=dst, send_sem=send, recv_sem=recv,
            device_id=device, device_id_type=MESH,
        )

    pad = jnp.zeros((8, D), F32)
    for b in range(2):
        mine[b] = jnp.concatenate([shard[b].astype(F32), pad], axis=0).astype(BF16)
    swap = remote(mine, sib, sib_send, sib_recv, sibling)
    swap.start()

    pick = quadrant_matrix(rowflag, leftflag).astype(BF16)
    places = jnp.dot(
        pick, regions[...].reshape(64, 16).astype(F32).astype(BF16), preferred_element_type=F32
    ).astype(jnp.int32)

    def prepare_frame(f):
        x = lat[f].astype(F32).reshape(64, D).astype(BF16)
        x = jnp.dot(pick, x, preferred_element_type=F32)
        y = layer_scale(x, mod[0, 0:1], mod[1, 0:1])
        x = x.astype(BF16)
        frame = lax.broadcasted_iota(jnp.int32, (64, 16), 1)
        label = jnp.sum(jnp.where(frame == f, places, 0), axis=1, keepdims=True)
        feats = features(label, 64)
        base = (f // 8) * 32 + f % 8
        for role in range(4):
            rows = slice(role * 16, role * 16 + 16)
            x0[base + role * 8] = x[rows]
            scaled[base + role * 8] = y[rows]
            for side in range(2):
                feat_q[side, base + role * 8] = feats[side][0][rows]
                feat_k[side, base + role * 8] = feats[side][1][rows]

    def prepare(i, _):
        prepare_frame(2 * i)
        prepare_frame(2 * i + 1)
        return 0

    lax.fori_loop(0, 3, prepare, 0)

    swap.wait()
    for b in range(2):
        own = mine[b].astype(F32)[:HD]
        theirs = sib[b].astype(F32)[:HD]
        low = jnp.where(core == 0, own, theirs)
        high = jnp.where(core == 0, theirs, own)
        pairs[b, chip] = jnp.concatenate([low, high], axis=0).astype(BF16)

    spans = ((0, 80), (80, 64))

    def x_copies(c, b):
        ref = pairs.at[b, chip, pl.ds(*spans[c])]
        return [
            remote(ref, ref, x_send.at[b, k], x_recv.at[b, k], along(k)[0]) for k in range(3)
        ]

    def row_chips(y):
        return [xx * 2 + y] + [((xx - k + 3) % 4) * 2 + y for k in range(3)]

    def flip_copies(c, b):
        out = []
        for k, source in enumerate(row_chips(ylo)):
            ref = pairs.at[b, source, pl.ds(*spans[c])]
            out.append(remote(ref, ref, flip_send.at[b, k], flip_recv.at[b, k], across[b]))
        return out

    def relay_copies(c, b):
        out = []
        for k, source in enumerate(row_chips(ylo)[1:] + row_chips(1 - ylo)):
            ref = pairs.at[b, source, pl.ds(*spans[c])]
            out.append(remote(ref, ref, rel_send.at[b, k], rel_recv.at[b, k], sibling))
        return out

    def by_core(act):
        for c in range(2):
            @pl.when(core == c)
            def _():
                act(c)

    def gather_start(b):
        def act(c):
            flip_copies(c, b)[0].start()
            for copy in x_copies(c, b):
                copy.start()
        by_core(act)

    def gather_turn(b):
        def act(c):
            flips, relays = flip_copies(c, b)[1:], relay_copies(c, b)[:3]
            for copy, flip, relay in zip(x_copies(c, b), flips, relays):
                copy.wait_recv()
                flip.start()
                relay.start()
        by_core(act)

    def gather_relay(b):
        def act(c):
            for flip, relay in zip(flip_copies(c, b), relay_copies(c, b)[3:]):
                flip.wait_recv()
                relay.start()
        by_core(act)

    def gather_end(b):
        def act(c):
            for relay in relay_copies(1 - c, b):
                relay.wait_recv()
        by_core(act)

    gather_start(0)
    lax.fori_loop(3, 8, prepare, 0)

    def triple(place, count, part):
        rows = scaled[place].reshape(count * 16, D)
        cols = pl.ds(pl.multiple_of(part * D, 128), D)
        out = jnp.dot(rows, wbuf[:, cols], preferred_element_type=F32)
        out = out * jnp.where(part == 0, SCALE, 1.0)
        qkv[place, :, cols] = out.astype(BF16).reshape(count, 16, D)

    def project(b, x, w):
        weight = pairs[b].reshape(D, D)
        branch = lax.dot_general(mixed[w].astype(BF16), weight, NT, preferred_element_type=F32)
        return (x.astype(F32) + mod[2, b : b + 1] * branch).astype(BF16).reshape(16, 16, D)

    for copy in loads(0):
        copy.wait()

    def make0(i, _):
        triple(pl.ds((i // 3) * 32, 32), 32, i % 3)
        return 0

    lax.fori_loop(0, 4, make0, 0)
    gather_turn(0)
    gather_start(1)
    lax.fori_loop(4, 6, make0, 0)
    for copy in loads(1):
        copy.start()

    def exchange(w, role):
        place = pl.ds(w * 32 + role * 8, 8)
        return remote(
            first.at[place], x1.at[place], out_send.at[w, role - 1], out_recv.at[w, role - 1],
            send_to[role],
        )

    def ahead(w, _):
        attend(qkv, w * 32, 1, feat_q, feat_k, mixed.at[w])

        @pl.when(w == 0)
        def _():
            gather_relay(0)
        return 0

    lax.fori_loop(0, 2, ahead, 0)
    gather_turn(1)
    gather_end(0)

    later = (1 - core) * jnp.where(depth == 0, 1 - rowflag, jnp.where(depth == 3, rowflag, 0))

    def far_pieces(w, _):
        here = pl.ds(w * 32 + 16, 16)
        first[here] = project(0, x0[here].reshape(256, D), w)
        exchange(w, VERT).start()

        @pl.when(later == 0)
        def _():
            exchange(w, DIAG).start()
        return 0

    lax.fori_loop(0, 2, far_pieces, 0)

    def near_pieces(w, _):
        base = w * 32
        attend(qkv, base, 0, feat_q, feat_k, mixed.at[w])
        out = project(0, x0[pl.ds(base, 16)].reshape(256, D), w)
        x1[pl.ds(base, 8)] = out[:8]
        first[pl.ds(base + 8, 8)] = out[8:]
        exchange(w, RIGHT).start()
        return 0

    lax.fori_loop(0, 2, near_pieces, 0)

    @pl.when(later == 1)
    def _():
        for w in range(2):
            exchange(w, DIAG).start()

    offset = shift[0]
    row_block = (ha + rowflag + 7) % 8
    at_row_end = jnp.where(row_block == 7, 1, 0)
    at_col_end = jnp.where(wa == 15, 1, 0)

    def label_tiles(i, _):
        w, role = i // 4, i % 4
        frame = w * 8 + lax.broadcasted_iota(jnp.int32, (128, 1), 0) // 16
        late = jnp.where(frame >= 16 - offset, w, 0)
        far = role // 2
        low = (far * rowflag + (1 - far) * (1 - rowflag)) * at_row_end
        feats = features(late * 4 + low * 2 + (role % 2) * at_col_end, 128)
        for side in range(2):
            feat_q[side, pl.ds(i * 8, 8)] = feats[side][0].reshape(8, 16, 128)
            feat_k[side, pl.ds(i * 8, 8)] = feats[side][1].reshape(8, 16, 128)
        return 0

    lax.fori_loop(0, 8, label_tiles, 0)

    for copy in loads(1):
        copy.wait()

    def norm(t, _):
        for k in range(2):
            place = pl.ds(t * 8 + k * 4, 4)
            x = x1[place].reshape(64, D).astype(F32)
            scaled[place] = layer_scale(x, mod[0, 1:2], mod[1, 1:2]).reshape(4, 16, D)
        return 0

    for chunk in (0, 1):
        def make1(w, _):
            for role in ((VERT, DIAG) if chunk == 1 else (RIGHT,)):
                exchange(w, role).wait_recv()
            start = w * 32 + chunk * 16
            lax.fori_loop(start // 8, start // 8 + 2, norm, 0)

            def part(p, _):
                triple(pl.ds(start, 16), 16, p)
                return 0

            lax.fori_loop(0, 3, part, 0)
            return 0

        lax.fori_loop(0, 2, make1, 0)
        if chunk == 0:
            gather_relay(1)

    by_z = core * jnp.where(depth == 3, 1 - rowflag, jnp.where(depth == 0, rowflag, 0))
    passes = core * jnp.where(depth == 2, 1 - rowflag, jnp.where(depth == 1, rowflag, 0))

    def give_back(w, role):
        place = pl.ds(w * 32 + role * 8, 8)
        return remote(
            second.at[place], result.at[place], back_send.at[w, role - 1],
            back_recv.at[w, role - 1], back_to[role],
        )

    def by_neighbour(w):
        place = pl.ds(w * 32 + DIAG * 8, 8)
        return remote(
            second.at[place], passed.at[w], pass_send.at[w], pass_recv.at[w], back_to[VERT]
        )

    def pass_back(w):
        place = pl.ds(w * 32 + DIAG * 8, 8)
        return remote(
            passed.at[w], result.at[place], pass_send.at[w], back_recv.at[w, DIAG - 1],
            back_to[RIGHT],
        )

    def keep(w):
        place = pl.ds(w * 32, 8)
        return pltpu.make_async_copy(second.at[place], result.at[place], own_sem.at[w])

    def roll(i, _):
        w, role = i // 4, i % 4
        for g in range(8):
            frame = (w * 8 + g + offset) % 16
            source = (frame // 8) * 32 + role * 8 + frame % 8
            rolled[i * 8 + g] = qkv[source]
            x0[i * 8 + g] = x1[source]
        return 0

    lax.fori_loop(0, 8, roll, 0)

    for chunk in (1, 0):
        def block1(w, _):
            base = w * 32
            attend(rolled, base, chunk, feat_q, feat_k, mixed.at[w])
            here = pl.ds(base + chunk * 16, 16)
            if chunk == 1:
                @pl.when(w == 0)
                def _():
                    gather_end(1)
            second[here] = project(1, x0[here].reshape(256, D), w)
            if chunk == 1:
                give_back(w, VERT).start()

                @pl.when(by_z == 1)
                def _():
                    by_neighbour(w).start()

                @pl.when(by_z == 0)
                def _():
                    give_back(w, DIAG).start()
            else:
                give_back(w, RIGHT).start()
                keep(w).start()
            return 0

        lax.fori_loop(0, 2, block1, 0)

    @pl.when(passes == 1)
    def _():
        for w in range(2):
            by_neighbour(w).wait_recv()
            pass_back(w).start()
        for w in range(2):
            pass_back(w).wait_send()

    for w in range(2):
        keep(w).wait()
        for role in (RIGHT, VERT, DIAG):
            exchange(w, role).wait_send()
            give_back(w, role).wait_recv()
        for role in (RIGHT, VERT):
            give_back(w, role).wait_send()

        @pl.when(by_z == 1)
        def _():
            by_neighbour(w).wait_send()

        @pl.when(by_z == 0)
        def _():
            give_back(w, DIAG).wait_send()

    def act(c):
        for b in range(2):
            for copy in x_copies(c, b) + flip_copies(c, b) + relay_copies(c, b):
                copy.wait_send()

    by_core(act)


def finish_body(shift, joined, out, tiles, final, in_sem, out_sem):
    back = quadrant_matrix(*corner_flags(lax.axis_index("wa"))).T.astype(BF16)

    def load(w, role):
        place = pl.ds(w * 32 + role * 8, 8)
        return pltpu.make_async_copy(joined.at[place], tiles.at[place], in_sem.at[w, role])

    for w in range(2):
        for role in range(4):
            load(w, role).start()

    def store(t):
        frame = (t + shift[0]) % 16
        return pltpu.make_async_copy(final.at[t], out.at[frame], out_sem.at[t])

    for w in range(2):
        for role in range(4):
            load(w, role).wait()

        for t in range(w * 8, w * 8 + 8):
            base = w * 32 + t % 8
            rows = jnp.concatenate([tiles[base + role * 8] for role in range(4)], axis=0)
            x = jnp.dot(back, rows, preferred_element_type=F32)
            final[t] = x.reshape(8, 8, D).astype(BF16)
            store(t).start()

    for t in range(16):
        store(t).wait()


def local(latent, qkv_weight, proj_weight, modulation, regions, frame_shift):
    vmem = pl.BlockSpec(memory_space=pltpu.VMEM)
    anywhere = pl.BlockSpec(memory_space=pl.ANY)
    smem = pl.BlockSpec(memory_space=pltpu.SMEM)
    tiles = pltpu.VMEM((64, 16, D), BF16)
    triples = pltpu.VMEM((64, 16, 3 * D), BF16)
    feats = pltpu.VMEM((2, 64, 16, 128), BF16)
    shards = pltpu.VMEM((2, 80, D), BF16)
    dma = pltpu.SemaphoreType.DMA
    joined = pl.pallas_call(
        body,
        out_shape=jax.ShapeDtypeStruct((64, 16, D), BF16),
        in_specs=[vmem, anywhere, vmem, vmem, vmem, smem],
        out_specs=anywhere,
        scratch_shapes=[
            pltpu.VMEM((D, 3 * D), BF16),
            tiles, tiles, tiles,
            triples, triples,
            pltpu.VMEM((2, 256, D), F32),
            tiles, tiles,
            pltpu.VMEM((2, 8, 16, D), BF16),
            feats, feats,
            shards, shards,
            pltpu.VMEM((2, 8, 2 * HD, D), BF16),
            dma((2, 3)),
            dma, dma,
            dma((2, 3)), dma((2, 3)), dma((2, 4)), dma((2, 4)), dma((2, 7)), dma((2, 7)),
            dma((2, 3)), dma((2, 3)), dma((2, 3)), dma((2, 3)),
            dma((2,)), dma((2,)), dma((2,)),
        ],
        compiler_params=pltpu.CompilerParams(
            collective_id=0, has_side_effects=True, vmem_limit_bytes=62 << 20
        ),
        name="blocks",
    )(
        latent,
        qkv_weight,
        jnp.swapaxes(proj_weight, 1, 2),
        jnp.swapaxes(modulation, 0, 1),
        jnp.transpose(regions, (1, 2, 0)),
        frame_shift,
    )
    return pl.pallas_call(
        finish_body,
        out_shape=jax.ShapeDtypeStruct((16, 8, 8, D), BF16),
        in_specs=[smem, anywhere],
        out_specs=anywhere,
        scratch_shapes=[tiles, pltpu.VMEM((16, 8, 8, D), BF16), dma((2, 4)), dma((16,))],
        compiler_params=pltpu.CompilerParams(vmem_limit_bytes=62 << 20),
        name="finish",
    )(frame_shift, joined)


def solution(mesh):
    in_specs = (P(None, "ha", "wa", None), P(), P(None, None, "wa"), P(), P(None, "ha", "wa"), P())
    out_specs = P(None, "ha", "wa", None)
    return jax.shard_map(local, mesh=mesh, in_specs=in_specs, out_specs=out_specs, check_vma=False)
```
